32 devices in a mesh: shot: 4 (over y, core), dom: 8 (over z, x).
Axes of the slice: x: 2, y: 2, z: 4, core: 2. Of those that a mesh axis runs over, the one named last changes fastest.
Arguments:
- model_slab: float32 [128, 128, 128], P('dom'), may hold values from 0.0225 to 0.17
- wave_prev: float32 [4, 128, 128, 128], P('shot', 'dom'), may hold values from -6 to 6
- wave_now: float32 [4, 128, 128, 128], P('shot', 'dom'), may hold values from -6 to 6
- adjoint_next: float32 [4, 128, 128, 128], P('shot', 'dom'), may hold values from -6 to 6
- adjoint_now: float32 [4, 128, 128, 128], P('shot', 'dom'), may hold values from -6 to 6
- wavelet: float32 [4, 8], P('shot'), may hold values from -12 to 12
- source_cell: int32 [4], P('shot'), may hold values from 0 to 2097151
- receiver_cells: int32 [4, 256], P('shot'), may hold values from 0 to 2097151
- observed: float32 [4, 8, 256], P('shot'), may hold values from -6 to 6
Outputs:
- direction: float32 [128, 128, 128], P('dom')
- new_model: float32 [128, 128, 128], P('dom')
The draws below stay inside these ranges and needn't reach their ends.
Inputs may be any that keep to these rules, and one draw needn't show every extreme that they name: `source_cell`: flat cell index x * 128 * 128 + y * 128 + z. `receiver_cells`: flat cell indices x * 128 * 128 + y * 128 + z; a cell may repeat.
All inputs are finite; a program needn't handle non-finite values. Where the reference program divides by a largest or mean magnitude, that divisor is 1e-20 or more.
Results may differ from the reference program's by a relative error of at most 0.000025.
Values sent between devices are 32-bit elements; how exact they have to be, the bound alone decides.
A program may use at most 192 MiB of HBM per device.

```python
import math
import jax
import jax.numpy as jnp
from jax import lax

NY = 128
NZ = 128
STEPS = 8
REC = 256
NX = 128
SHOTS = 4


def plant(array, rng, smallest, top_value):
    longest = array.shape.index(max(array.shape))
    spots = []
    for shift in (0, 1):
        where = [jax.random.randint(jax.random.fold_in(rng, axis), (), 0, length) for axis, length in enumerate(array.shape)]
        where[longest] = (where[longest] + shift) % array.shape[longest]
        spots.append(tuple(where))
    return array.at[spots[0]].set(smallest).at[spots[1]].set(top_value)


def levels(key, extent, cuts, least, largest):
    def one(axis_at, blocks):
        heights = jax.random.uniform(jax.random.fold_in(jax.random.fold_in(key, 6), axis_at), (blocks,), jnp.float32, least / len(cuts), largest / len(cuts))
        return jnp.repeat(jnp.exp(heights), extent[axis_at] // blocks).reshape((-1,) + (1,) * (len(extent) - axis_at - 1))

    loudness = one(*cuts[0])
    for cut in cuts[1:]:
        loudness = loudness * one(*cut)
    return loudness


def scatter_about(rng, extent, deviation, bound, split=(), kind=jnp.bfloat16):
    result = deviation * jax.random.normal(rng, extent, jnp.float32)
    if split:
        result = result * levels(rng, extent, split, -0.22, 0.18)
    return jnp.clip(result, -bound, bound).astype(kind)


def setup_inputs(seed: int = 0) -> dict:
    streams_of = jax.random.split(jax.random.key(seed), 10)
    return {
        "model_slab": jnp.clip(jnp.exp(math.log(0.17) - 2.022283 * jax.random.uniform(streams_of[0], (NX, NY, NZ), jnp.float32) ** levels(streams_of[0], (NX, NY, NZ), ((0, 8),), -0.2, 0.2)), 0.0225, 0.17),
        "wave_prev": scatter_about(streams_of[1], (SHOTS, NX, NY, NZ), 1.0, 6.0, ((0, 4), (1, 8)), jnp.float32),
        "wave_now": scatter_about(streams_of[2], (SHOTS, NX, NY, NZ), 1.0, 6.0, ((0, 4), (1, 8)), jnp.float32),
        "adjoint_next": scatter_about(streams_of[3], (SHOTS, NX, NY, NZ), 1.0, 6.0, ((0, 4), (1, 8)), jnp.float32),
        "adjoint_now": scatter_about(streams_of[4], (SHOTS, NX, NY, NZ), 1.0, 6.0, ((0, 4), (1, 8)), jnp.float32),
        "wavelet": scatter_about(streams_of[5], (SHOTS, STEPS), 3.0, 12.0, ((0, 4),), jnp.float32),
        "source_cell": plant(jax.random.randint(streams_of[6], (SHOTS,), 0, NX * NY * NZ), jax.random.fold_in(streams_of[6], 1), 0, (NX * NY * NZ) - 1).astype(jnp.int32),
        "receiver_cells": plant(jax.random.randint(streams_of[7], (SHOTS, REC), 0, NX * NY * NZ), jax.random.fold_in(streams_of[7], 1), 0, (NX * NY * NZ) - 1).astype(jnp.int32),
        "observed": scatter_about(streams_of[8], (SHOTS, STEPS, REC), 1.0, 6.0, ((0, 4),), jnp.float32),
    }


COEFFS = (8.0 / 5.0, -1.0 / 5.0, 8.0 / 315.0, -1.0 / 560.0)
CENTRE = -205.0 / 72.0
STEP_FRACTION = 0.1
EPSILON = 1e-6


def shifted(field, axis, offset):
    length = field.shape[axis]
    filler_shape = list(field.shape)
    filler_shape[axis] = abs(offset)
    filler = jnp.zeros(filler_shape, field.dtype)
    if offset > 0:
        return jnp.concatenate([lax.slice_in_dim(field, offset, length, axis=axis), filler], axis)
    return jnp.concatenate([filler, lax.slice_in_dim(field, 0, length + offset, axis=axis)], axis)


def laplace(field):
    total = (3.0 * CENTRE) * field
    for axis in (0, 1, 2):
        for index, weight in enumerate(COEFFS):
            offset = index + 1
            total = total + weight * (shifted(field, axis, offset) + shifted(field, axis, -offset))
    return total


def one_shot(model_slab, wave_prev, wave_now, adjoint_next, adjoint_now, wavelet_row, source_one, receivers, observed_rows):
    shape = wave_now.shape
    images = []
    residuals = []
    older, current = wave_prev, wave_now
    for tick in range(STEPS):
        image = laplace(current)
        newer = 2.0 * current - older + model_slab * image
        newer = newer.reshape(-1).at[source_one].add(wavelet_row[tick]).reshape(shape)
        residuals.append(newer.reshape(-1)[receivers] - observed_rows[tick])
        images.append(image)
        older, current = current, newer
    later, present = adjoint_next, adjoint_now
    gradient = jnp.zeros(shape, jnp.float32)
    for tick in reversed(range(STEPS)):
        earlier = 2.0 * present - later + model_slab * laplace(present)
        earlier = earlier.reshape(-1).at[receivers].add(residuals[tick]).reshape(shape)
        gradient = gradient + earlier * images[tick]
        later, present = present, earlier
    return gradient


def reference(model_slab, wave_prev, wave_now, adjoint_next, adjoint_now, wavelet, source_cell, receiver_cells, observed):
    def accumulate(total, items):
        return total + one_shot(model_slab, *items), None

    start = jnp.zeros(model_slab.shape, jnp.float32)
    total, unused = lax.scan(accumulate, start, (wave_prev, wave_now, adjoint_next, adjoint_now, wavelet, source_cell, receiver_cells, observed))
    peak = jnp.max(jnp.abs(total))
    direction = total / (peak + EPSILON)
    new_model = model_slab * (1.0 - STEP_FRACTION * direction)
    return direction, new_model
```

```python
import functools
import math

import jax
import jax.numpy as jnp
from jax import lax
from jax.experimental import pallas as pl
from jax.experimental.pallas import tpu as pltpu
from jax.sharding import PartitionSpec as P

STEPS = 8
COEFFS = (8.0 / 5.0, -1.0 / 5.0, 8.0 / 315.0, -1.0 / 560.0)
CENTRE = -205.0 / 72.0
BAND = (8064.0, -1008.0, 128.0, -9.0)
BAND_SCALE = 1.0 / 5040.0
STEP_FRACTION = 0.1
EPSILON = 1e-06
MESH = pl.DeviceIdType.MESH
F32, BF16 = jnp.float32, jnp.bfloat16


def pieces(value):
    high = value.astype(BF16)
    rest = value - high.astype(F32)
    middle = rest.astype(BF16)
    low = (rest - middle.astype(F32)).astype(BF16)
    return high, middle, low


def kernel(
    shots, doms,
    pack_in, model_in, wprev_in, wnow_in, anext_in, anow_in,
    direction_ref, new_model_ref,
    wave, adj, images, sources, counts, model, grad, pack, targets, band, spot, other, parts, total,
    own_model, tops,
    swap_send, swap_recv, halo_send, halo_recv, far_send, far_recv, model_send, model_recv,
    sum_send, sum_recv, part_send, part_recv, all_send, all_recv, core_send, core_recv,
    top_send, top_recv, own_sem,
):
    rows, ny, nz = model.shape
    rec = pack.shape[2]
    shot, dom = lax.axis_index("shot"), lax.axis_index("dom")
    group, core = shot // 2, shot % 2
    pair, half = dom // 2, dom % 2
    groups = shots // 2
    chunk = rows // groups
    pieces_of = math.gcd(4, chunk)
    depth = chunk // pieces_of
    slab = 2 * pair + core
    moves = core != half
    stays = core == half
    partner = {"shot": 2 * group + (1 - core), "dom": 2 * pair + (1 - half)}
    across = {"shot": shot, "dom": 2 * pair + (1 - half)}
    beside = {"shot": 2 * group + (1 - core), "dom": dom}
    far_side, near_side = core, 1 - core

    def has(side):
        return jnp.where(side == 0, slab > 0, slab < doms - 1)

    def toward(side):
        step = jnp.where(side == core, jnp.where(side == 0, -2, 2), 0)
        return {"shot": 2 * group + (1 - core), "dom": dom + step}

    for buf in (wave, adj):
        def clear(i, carry, buf=buf):
            for slot in range(2):
                buf[slot, i, 0:8, :] = jnp.zeros((8, nz), F32)
                buf[slot, i, ny + 8 : ny + 16, :] = jnp.zeros((8, nz), F32)
            return carry

        lax.fori_loop(0, rows + 8, clear, 0)

        def clear_halo(i, carry, buf=buf):
            for slot in range(2):
                buf[slot, i, 8 : ny + 8, :] = jnp.zeros((ny, nz), F32)
                buf[slot, rows + 4 + i, 8 : ny + 8, :] = jnp.zeros((ny, nz), F32)
            return carry

        lax.fori_loop(0, 4, clear_halo, 0)

    barrier = pltpu.get_barrier_semaphore()

    def greet(device):
        pl.semaphore_signal(barrier, inc=1, device_id=device, device_id_type=MESH)

    def member(n):
        return {"shot": 2 * group + n % 2, "dom": n // 2}

    me = 2 * dom + core

    def meet(n, carry):
        @pl.when(n != me)
        def _():
            greet(member(n))

        return carry

    lax.fori_loop(0, 2 * doms, meet, 0)
    for o in range(1, groups):
        greet({"shot": 2 * lax.rem(group + o, groups) + core, "dom": dom})
    pl.semaphore_wait(barrier, 2 * doms - 1 + groups - 1)

    def block(ref, index):
        return ref.at[pl.ds(index * chunk, chunk)]

    def own(buf, slot):
        return buf.at[slot, pl.ds(4, rows), pl.ds(8, ny), :]

    swaps = (
        (pack_in, pack),
        (wnow_in, own(wave, 0)),
        (wprev_in, own(wave, 1)),
        (model_in, model),
        (anow_in, own(adj, 0)),
        (anext_in, own(adj, 1)),
    )

    def remote(i):
        src, dst = swaps[i]
        if i == 3:
            src, dst = block(src, group), block(dst, group)
        return pltpu.make_async_remote_copy(
            src_ref=src, dst_ref=dst, send_sem=swap_send.at[i], recv_sem=swap_recv.at[i],
            device_id=partner, device_id_type=MESH,
        )

    def local(i):
        src, dst = swaps[i]
        return pltpu.make_async_copy(src, dst, swap_recv.at[i])

    def fetch(*items):
        @pl.when(moves)
        def _():
            for i in items:
                remote(i).start()

        @pl.when(stays)
        def _():
            for i in items:
                local(i).start()

    def fetched(*items):
        @pl.when(moves)
        def _():
            for i in items:
                remote(i).wait()

        @pl.when(stays)
        def _():
            for i in items:
                local(i).wait()

    fetch(0, 1, 3, 2)
    keep_model = pltpu.make_async_copy(model_in, own_model, own_sem.at[0])
    keep_model.start()

    shape = (2 * nz, nz)
    distance = jnp.abs(
        lax.broadcasted_iota(jnp.int32, shape, 0) % nz - lax.broadcasted_iota(jnp.int32, shape, 1)
    )
    weights = jnp.zeros(shape, F32)
    for index, weight in enumerate(BAND):
        weights = jnp.where(distance == index + 1, weight, weights)
    band[...] = weights.astype(BF16)

    def clear_grad(i, carry):
        grad[i] = jnp.zeros((ny, nz), F32)
        return carry

    lax.fori_loop(0, rows, clear_grad, 0)

    fetched(0)

    spots_z = pack[STEPS + 1, 1:2, :]
    columns = lax.broadcasted_iota(jnp.int32, (nz, rec), 0).astype(F32) == spots_z

    def place(q, carry):
        for index, piece in enumerate(pieces(pack[q, 0:1, :])):
            targets[q, :, index * rec : (index + 1) * rec] = jnp.where(
                columns, piece.astype(F32), 0.0
            ).astype(BF16)
        return carry

    lax.fori_loop(0, STEPS + 1, place, 0)

    def spread(i, carry):
        line = lax.broadcasted_iota(jnp.int32, (ny, rec), 0) + (slab * rows + i) * ny
        hit = jnp.where(line.astype(F32) == pack[STEPS + 1, 0:1, :], 1.0, 0.0).astype(BF16)
        hits = jnp.concatenate([hit, hit, hit], axis=1)

        def amount(q):
            return lax.dot_general(
                hits, targets[q], (((1,), (1,)), ((), ())), preferred_element_type=F32
            )

        def one(q, carry):
            sources[q, i] = amount(q)
            return carry

        lax.fori_loop(0, STEPS, one, 0)
        counts[i] = amount(STEPS)
        return carry

    lax.fori_loop(0, rows, spread, 0)
    spot[...] = jnp.where(
        (lax.broadcasted_iota(jnp.int32, (ny, nz), 0).astype(F32) == pack[STEPS + 1, 3:4, 0:nz])
        & (lax.broadcasted_iota(jnp.int32, (ny, nz), 1).astype(F32) == pack[STEPS + 1, 4:5, 0:nz]),
        1.0,
        0.0,
    )

    def face(buf, field, u, side):
        slot = lax.rem(u, 2)
        src = jnp.where(side == 0, 4, rows)
        dst = jnp.where(side == 0, rows + 4, 0)
        return pltpu.make_async_remote_copy(
            src_ref=buf.at[slot, pl.ds(src, 4), pl.ds(8, ny), :],
            dst_ref=buf.at[slot, pl.ds(dst, 4), pl.ds(8, ny), :],
            send_sem=halo_send.at[field, u, side],
            recv_sem=halo_recv.at[field, u, 1 - side],
            device_id=toward(side),
            device_id_type=MESH,
        )

    def arrival(buf, field, u, side):
        slot = lax.rem(u, 2)
        dst = jnp.where(side == 0, 0, rows + 4)
        block = buf.at[slot, pl.ds(dst, 4), pl.ds(8, ny), :]
        return pltpu.make_async_remote_copy(
            src_ref=block, dst_ref=block,
            send_sem=halo_send.at[field, u, side],
            recv_sem=halo_recv.at[field, u, side],
            device_id=toward(side),
            device_id_type=MESH,
        )

    def layer(buf, field, u, j):
        slot = lax.rem(u, 2)
        src = jnp.where(far_side == 0, 4 + j, rows + 3 - j)
        dst = jnp.where(far_side == 0, rows + 4 + j, 3 - j)
        return pltpu.make_async_remote_copy(
            src_ref=buf.at[slot, src, pl.ds(8, ny), :],
            dst_ref=buf.at[slot, dst, pl.ds(8, ny), :],
            send_sem=far_send.at[field, u, j],
            recv_sem=far_recv.at[field, u, j],
            device_id=toward(far_side),
            device_id_type=MESH,
        )

    def layer_arrival(buf, field, u, j):
        slot = lax.rem(u, 2)
        dst = jnp.where(far_side == 0, 3 - j, rows + 4 + j)
        place = buf.at[slot, dst, pl.ds(8, ny), :]
        return pltpu.make_async_remote_copy(
            src_ref=place, dst_ref=place,
            send_sem=far_send.at[field, u, j],
            recv_sem=far_recv.at[field, u, j],
            device_id=toward(far_side),
            device_id_type=MESH,
        )

    def send_near(buf, field, u):
        @pl.when(has(near_side))
        def _():
            face(buf, field, u, near_side).start()

    def send_all(buf, field):
        @pl.when(has(far_side))
        def _():
            for j in range(4):
                layer(buf, field, 0, j).start()

        send_near(buf, field, 0)

    def laplace(buf, slot, i):
        field = buf[slot, 4 + i, 8 : 8 + ny, :]
        image = (3.0 * CENTRE) * field
        for index, weight in enumerate(COEFFS):
            k = index + 1
            image = image + weight * (
                (buf[slot, 4 + i + k, 8 : 8 + ny, :] + buf[slot, 4 + i - k, 8 : 8 + ny, :])
                + (buf[slot, 4 + i, 8 + k : 8 + k + ny, :] + buf[slot, 4 + i, 8 - k : 8 - k + ny, :])
            )
        high, middle, low = pieces(field)
        along = jnp.dot(
            jnp.concatenate([high, middle], axis=1), band[...], preferred_element_type=F32
        ) + jnp.dot(low, band[0:nz, :], preferred_element_type=F32)
        return field, image + along * BAND_SCALE

    def advance(buf, field, u, plane):
        slot = lax.rem(u, 2)

        def run(first, count):
            lax.fori_loop(first, first + count, lambda i, carry: (plane(u, slot, i), carry)[1], 0)

        run(4, rows - 8)

        @pl.when(has(near_side))
        def _():
            arrival(buf, field, u, near_side).wait_recv()

            @pl.when(u > 0)
            def _():
                face(buf, field, u - 1, near_side).wait_send()

        run(jnp.where(near_side == 0, 0, rows - 4), 4)

        @pl.when(u < STEPS - 1)
        def _():
            send_near(buf, field, u + 1)

        even = lax.rem(u, 2) == 0

        def one(n, carry):
            j = jnp.where(even, 3 - n, n)

            @pl.when(has(far_side))
            def _():
                @pl.when(even)
                def _():
                    layer_arrival(buf, field, u, n).wait_recv()

                @pl.when(jnp.logical_and(jnp.logical_not(even), n == 0))
                def _():
                    for m in (3, 2, 1, 0):
                        layer_arrival(buf, field, u, m).wait_recv()

                @pl.when(u > 0)
                def _():
                    layer(buf, field, u - 1, j).wait_send()

            plane(u, slot, jnp.where(far_side == 0, j, rows - 1 - j))

            @pl.when(jnp.logical_and(has(far_side), u < STEPS - 1))
            def _():
                layer(buf, field, u + 1, j).start()

            return carry

        lax.fori_loop(0, 4, one, 0)

    def settle(buf, field):
        @pl.when(has(near_side))
        def _():
            face(buf, field, STEPS - 1, near_side).wait_send()

        @pl.when(has(far_side))
        def _():
            for j in range(4):
                layer(buf, field, STEPS - 1, j).wait_send()

    def wave_plane(t, slot, i):
        now, image = laplace(wave, slot, i)
        position = (slab * rows + i).astype(F32)
        push = jnp.where(pack[STEPS + 1, 2:3, 0:nz] == position, pack[t, 1:2, 0:nz], 0.0)
        new = (
            2.0 * now - wave[1 - slot, 4 + i, 8 : 8 + ny, :] + model[i] * image + push * spot[...]
        )
        wave[1 - slot, 4 + i, 8 : 8 + ny, :] = new
        images[t, i] = image
        sources[t, i] = counts[i] * new - sources[t, i]

    def adjoint_plane(u, slot, i):
        t = STEPS - 1 - u
        now, image = laplace(adj, slot, i)
        new = 2.0 * now - adj[1 - slot, 4 + i, 8 : 8 + ny, :] + model[i] * image + sources[t, i]
        adj[1 - slot, 4 + i, 8 : 8 + ny, :] = new
        grad[i] = grad[i] + new * images[t, i]

    fetched(1)
    send_all(wave, 0)
    fetched(3)

    def model_part(o, index, peer):
        return pltpu.make_async_remote_copy(
            src_ref=block(model, index), dst_ref=block(model, index),
            send_sem=model_send.at[o - 1], recv_sem=model_recv.at[o - 1],
            device_id={"shot": 2 * peer + core, "dom": dom}, device_id_type=MESH,
        )

    @pl.when(moves)
    def _():
        for o in range(1, groups):
            model_part(o, group, lax.rem(group + o, groups)).start()

    fetched(2)
    fetch(4, 5)

    @pl.when(moves)
    def _():
        for o in range(1, groups):
            origin = lax.rem(group + groups - o, groups)
            model_part(o, origin, origin).wait_recv()
            model_part(o, group, lax.rem(group + o, groups)).wait_send()

    def forward(t, carry):
        @pl.when(t == STEPS - 1)
        def _():
            fetched(4, 5)
            send_all(adj, 1)

        advance(wave, 0, t, wave_plane)
        return carry

    lax.fori_loop(0, STEPS, forward, 0)
    settle(wave, 0)

    def backward(u, carry):
        advance(adj, 1, u, adjoint_plane)
        return carry

    lax.fori_loop(0, STEPS, backward, 0)
    settle(adj, 1)

    def part(ref, index, n):
        return ref.at[pl.ds(index * chunk + n * depth, depth)]

    def to_across(q, n):
        return pltpu.make_async_remote_copy(
            src_ref=part(grad, q, n), dst_ref=part(other, q, n),
            send_sem=sum_send.at[q, n], recv_sem=sum_recv.at[q, n],
            device_id=across, device_id_type=MESH,
        )

    def to_group(o, n):
        peer = lax.rem(group + o, groups)
        return pltpu.make_async_remote_copy(
            src_ref=part(grad, peer, n), dst_ref=part(parts.at[o - 1], 0, n),
            send_sem=part_send.at[o - 1, n], recv_sem=part_recv.at[o - 1, n],
            device_id={"shot": 2 * peer + core, "dom": dom}, device_id_type=MESH,
        )

    def share(o, n, index, peer):
        return pltpu.make_async_remote_copy(
            src_ref=part(total, index, n), dst_ref=part(total, index, n),
            send_sem=all_send.at[o - 1, n], recv_sem=all_recv.at[o - 1, n],
            device_id={"shot": 2 * peer + core, "dom": dom}, device_id_type=MESH,
        )

    def to_core(o, n):
        index = lax.rem(group + groups - o, groups)
        return pltpu.make_async_remote_copy(
            src_ref=part(total, index, n), dst_ref=part(total, index, n),
            send_sem=core_send.at[o, n], recv_sem=core_recv.at[o, n],
            device_id=beside, device_id_type=MESH,
        )

    def top(n):
        return pltpu.make_async_remote_copy(
            src_ref=tops.at[dom], dst_ref=tops.at[dom],
            send_sem=top_send.at[n], recv_sem=top_recv.at[dom],
            device_id=member(n), device_id_type=MESH,
        )

    def top_arrival(d):
        return pltpu.make_async_remote_copy(
            src_ref=tops.at[d], dst_ref=tops.at[d],
            send_sem=top_send.at[0], recv_sem=top_recv.at[d],
            device_id=beside, device_id_type=MESH,
        )

    keep_model.wait()

    @pl.when(moves)
    def _():
        for n in range(pieces_of):
            for o in list(range(1, groups)) + [0]:
                to_across(lax.rem(group + o, groups), n).start()
        for n in range(pieces_of):
            to_core(0, n).wait_recv()
        for o in range(1, groups):
            for n in range(pieces_of):
                to_core(o, n).wait_recv()
        for n in range(pieces_of):
            for o in range(groups):
                to_across(o, n).wait_send()

    @pl.when(stays)
    def _():
        for n in range(pieces_of + 1):
            if n < pieces_of:
                for o in range(1, groups):
                    index = lax.rem(group + o, groups)
                    to_across(index, n).wait_recv()
                    for m in range(n * depth, n * depth + depth):
                        i = index * chunk + m
                        grad[i] = grad[i] + other[i]
                    to_group(o, n).start()
            if n > 0:
                last = n - 1
                to_across(group, last).wait_recv()
                for o in range(1, groups):
                    to_group(o, last).wait_recv()
                for m in range(last * depth, last * depth + depth):
                    i = group * chunk + m
                    value = grad[i] + other[i]
                    for o in range(1, groups):
                        value = value + parts[o - 1, m]
                    total[i] = value
                for o in range(1, groups):
                    share(o, last, group, lax.rem(group + o, groups)).start()
                to_core(0, last).start()
        for o in range(1, groups):
            origin = lax.rem(group + groups - o, groups)
            for n in range(pieces_of):
                share(o, n, origin, origin).wait_recv()
                to_core(o, n).start()

        def largest(i, best):
            return jnp.maximum(best, jnp.max(jnp.abs(total[i]).reshape(ny // 8, 8, nz), axis=0))

        tops[dom] = lax.fori_loop(0, rows, largest, jnp.zeros((8, nz), F32))

        def tell(n, carry):
            @pl.when(n != me)
            def _():
                top(n).start()

            return carry

        lax.fori_loop(0, 2 * doms, tell, 0)

    def hear(d, carry):
        @pl.when(jnp.logical_or(d != dom, moves))
        def _():
            top_arrival(d).wait_recv()

        return carry

    lax.fori_loop(0, doms, hear, 0)
    best = lax.fori_loop(0, doms, lambda d, b: jnp.maximum(b, tops[d]), jnp.zeros((8, nz), F32))
    divisor = jnp.max(best, keepdims=True) + EPSILON

    def finish(i, carry):
        direction = total[i] / divisor
        direction_ref[i] = direction
        new_model_ref[i] = own_model[i] * (1.0 - STEP_FRACTION * direction)
        return carry

    lax.fori_loop(0, rows, finish, 0)

    @pl.when(stays)
    def _():
        def told(n, carry):
            @pl.when(n != me)
            def _():
                top(n).wait_send()

            return carry

        lax.fori_loop(0, 2 * doms, told, 0)
        for n in range(pieces_of):
            for o in range(1, groups):
                to_group(o, n).wait_send()
                share(o, n, group, lax.rem(group + o, groups)).wait_send()
            for o in range(groups):
                to_core(o, n).wait_send()


def packed(rows, ny, nz, wavelet, source_cell, receiver_cells, observed):
    rec = receiver_cells.shape[1]
    zeros = jnp.zeros((STEPS, rec), F32)
    steps = jnp.stack(
        [observed[0], jnp.broadcast_to(wavelet[0][:, None], (STEPS, rec))] + [zeros] * 6, axis=1
    )
    cell = jnp.broadcast_to(source_cell[0], (rec,))
    receivers = receiver_cells[0]
    ones = jnp.stack([jnp.ones((rec,), F32)] + [zeros[0]] * 7)
    places = [receivers // nz, receivers % nz, cell // (ny * nz), cell // nz % ny, cell % nz]
    places = jnp.stack([p.astype(F32) for p in places] + [zeros[0]] * 3)
    return jnp.concatenate([steps, ones[None], places[None]], axis=0)


def on_device(
    shots, doms, model_slab, wave_prev, wave_now, adjoint_next, adjoint_now,
    wavelet, source_cell, receiver_cells, observed,
):
    rows, ny, nz = model_slab.shape
    rec = receiver_cells.shape[1]
    groups = shots // 2
    pack = packed(rows, ny, nz, wavelet, source_cell, receiver_cells, observed)
    dma = pltpu.SemaphoreType.DMA
    padded = (2, rows + 8, ny + 16, nz)
    slab = (rows, ny, nz)
    pieces_of = math.gcd(4, rows // groups)
    return pl.pallas_call(
        functools.partial(kernel, shots, doms),
        out_shape=(jax.ShapeDtypeStruct(slab, F32),) * 2,
        in_specs=[pl.BlockSpec(memory_space=pl.ANY)] * 6,
        out_specs=(pl.BlockSpec(memory_space=pltpu.VMEM),) * 2,
        scratch_shapes=[
            pltpu.VMEM(padded, F32),
            pltpu.VMEM(padded, F32),
            pltpu.VMEM((STEPS,) + slab, F32),
            pltpu.VMEM((STEPS,) + slab, F32),
            pltpu.VMEM(slab, F32),
            pltpu.VMEM(slab, F32),
            pltpu.VMEM(slab, F32),
            pltpu.VMEM(pack.shape, F32),
            pltpu.VMEM((STEPS + 1, nz, 3 * rec), BF16),
            pltpu.VMEM((2 * nz, nz), BF16),
            pltpu.VMEM((ny, nz), F32),
            pltpu.VMEM(slab, F32),
            pltpu.VMEM((groups - 1, rows // groups, ny, nz), F32),
            pltpu.VMEM(slab, F32),
            pltpu.VMEM(slab, F32),
            pltpu.VMEM((doms, 8, nz), F32),
            dma((6,)),
            dma((6,)),
            dma((2, STEPS, 2)),
            dma((2, STEPS, 2)),
            dma((2, STEPS, 4)),
            dma((2, STEPS, 4)),
            dma((groups - 1,)),
            dma((groups - 1,)),
            dma((groups, pieces_of)),
            dma((groups, pieces_of)),
            dma((groups - 1, pieces_of)),
            dma((groups - 1, pieces_of)),
            dma((groups - 1, pieces_of)),
            dma((groups - 1, pieces_of)),
            dma((groups, pieces_of)),
            dma((groups, pieces_of)),
            dma((2 * doms,)),
            dma((doms,)),
            dma((1,)),
        ],
        compiler_params=pltpu.CompilerParams(
            collective_id=0, has_side_effects=True, vmem_limit_bytes=48 * 1024 * 1024
        ),
    )(pack, model_slab, wave_prev[0], wave_now[0], adjoint_next[0], adjoint_now[0])


def solution(mesh):
    placed = (
        P("dom", None, None),
        P("shot", "dom", None, None),
        P("shot", "dom", None, None),
        P("shot", "dom", None, None),
        P("shot", "dom", None, None),
        P("shot", None),
        P("shot"),
        P("shot", None),
        P("shot", None, None),
    )
    return jax.shard_map(
        functools.partial(on_device, mesh.shape["shot"], mesh.shape["dom"]),
        mesh=mesh,
        in_specs=placed,
        out_specs=(P("dom", None, None), P("dom", None, None)),
        check_vma=False,
    )
```

```python
import functools
import math

import jax
import jax.numpy as jnp
from jax import lax
from jax.experimental import pallas as pl
from jax.experimental.pallas import tpu as pltpu
from jax.sharding import PartitionSpec as P

STEPS = 8
COEFFS = (8.0 / 5.0, -1.0 / 5.0, 8.0 / 315.0, -1.0 / 560.0)
CENTRE = -205.0 / 72.0
BAND = (8064.0, -1008.0, 128.0, -9.0)
BAND_SCALE = 1.0 / 5040.0
STEP_FRACTION = 0.1
EPSILON = 1e-06
MESH = pl.DeviceIdType.MESH
F32, BF16 = jnp.float32, jnp.bfloat16


def pieces(value):
    high = value.astype(BF16)
    rest = value - high.astype(F32)
    middle = rest.astype(BF16)
    low = (rest - middle.astype(F32)).astype(BF16)
    return high, middle, low


def kernel(
    shots, doms,
    pack_in, model_in, wprev_in, wnow_in, anext_in, anow_in,
    direction_ref, new_model_ref,
    wave, adj, images, sources, counts, model, grad, pack, targets, band, spot, other, parts, total,
    own_model, tops,
    swap_send, swap_recv, halo_send, halo_recv, far_send, far_recv, model_send, model_recv,
    sum_send, sum_recv, part_send, part_recv, all_send, all_recv, core_send, core_recv,
    top_send, top_recv, own_sem,
):
    rows, ny, nz = model.shape
    rec = pack.shape[2]
    shot, dom = lax.axis_index("shot"), lax.axis_index("dom")
    group, core = shot // 2, shot % 2
    pair, half = dom // 2, dom % 2
    groups = shots // 2
    chunk = rows // groups
    pieces_of = math.gcd(4, chunk)
    depth = chunk // pieces_of
    slab = 2 * pair + core
    moves = core != half
    stays = core == half
    partner = {"shot": 2 * group + (1 - core), "dom": 2 * pair + (1 - half)}
    across = {"shot": shot, "dom": 2 * pair + (1 - half)}
    beside = {"shot": 2 * group + (1 - core), "dom": dom}
    far_side, near_side = core, 1 - core

    def has(side):
        return jnp.where(side == 0, slab > 0, slab < doms - 1)

    def toward(side):
        step = jnp.where(side == core, jnp.where(side == 0, -2, 2), 0)
        return {"shot": 2 * group + (1 - core), "dom": dom + step}

    for buf in (wave, adj):
        def clear(i, carry, buf=buf):
            for slot in range(2):
                buf[slot, i, 0:8, :] = jnp.zeros((8, nz), F32)
                buf[slot, i, ny + 8 : ny + 16, :] = jnp.zeros((8, nz), F32)
            return carry

        lax.fori_loop(0, rows + 8, clear, 0)

        def clear_halo(i, carry, buf=buf):
            for slot in range(2):
                buf[slot, i, 8 : ny + 8, :] = jnp.zeros((ny, nz), F32)
                buf[slot, rows + 4 + i, 8 : ny + 8, :] = jnp.zeros((ny, nz), F32)
            return carry

        lax.fori_loop(0, 4, clear_halo, 0)

    barrier = pltpu.get_barrier_semaphore()

    def greet(device):
        pl.semaphore_signal(barrier, inc=1, device_id=device, device_id_type=MESH)

    def member(n):
        return {"shot": 2 * group + n % 2, "dom": n // 2}

    me = 2 * dom + core

    def meet(n, carry):
        @pl.when(n != me)
        def _():
            greet(member(n))

        return carry

    lax.fori_loop(0, 2 * doms, meet, 0)
    for o in range(1, groups):
        greet({"shot": 2 * lax.rem(group + o, groups) + core, "dom": dom})
    pl.semaphore_wait(barrier, 2 * doms - 1 + groups - 1)

    def block(ref, index):
        return ref.at[pl.ds(index * chunk, chunk)]

    def own(buf, slot):
        return buf.at[slot, pl.ds(4, rows), pl.ds(8, ny), :]

    swaps = (
        (pack_in, pack),
        (wnow_in, own(wave, 0)),
        (wprev_in, own(wave, 1)),
        (model_in, model),
        (anow_in, own(adj, 0)),
        (anext_in, own(adj, 1)),
    )

    def remote(i):
        src, dst = swaps[i]
        if i == 3:
            src, dst = block(src, group), block(dst, group)
        return pltpu.make_async_remote_copy(
            src_ref=src, dst_ref=dst, send_sem=swap_send.at[i], recv_sem=swap_recv.at[i],
            device_id=partner, device_id_type=MESH,
        )

    def local(i):
        src, dst = swaps[i]
        return pltpu.make_async_copy(src, dst, swap_recv.at[i])

    def fetch(*items):
        @pl.when(moves)
        def _():
            for i in items:
                remote(i).start()

        @pl.when(stays)
        def _():
            for i in items:
                local(i).start()

    def fetched(*items):
        @pl.when(moves)
        def _():
            for i in items:
                remote(i).wait()

        @pl.when(stays)
        def _():
            for i in items:
                local(i).wait()

    fetch(0, 1, 3, 2)
    keep_model = pltpu.make_async_copy(model_in, own_model, own_sem.at[0])
    keep_model.start()

    shape = (2 * nz, nz)
    distance = jnp.abs(
        lax.broadcasted_iota(jnp.int32, shape, 0) % nz - lax.broadcasted_iota(jnp.int32, shape, 1)
    )
    weights = jnp.zeros(shape, F32)
    for index, weight in enumerate(BAND):
        weights = jnp.where(distance == index + 1, weight, weights)
    band[...] = weights.astype(BF16)

    def clear_grad(i, carry):
        grad[i] = jnp.zeros((ny, nz), F32)
        return carry

    lax.fori_loop(0, rows, clear_grad, 0)

    fetched(0)

    spots_z = pack[STEPS + 1, 1:2, :]
    columns = lax.broadcasted_iota(jnp.int32, (nz, rec), 0).astype(F32) == spots_z

    def place(q, carry):
        for index, piece in enumerate(pieces(pack[q, 0:1, :])):
            targets[q, :, index * rec : (index + 1) * rec] = jnp.where(
                columns, piece.astype(F32), 0.0
            ).astype(BF16)
        return carry

    lax.fori_loop(0, STEPS + 1, place, 0)

    def spread(i, carry):
        line = lax.broadcasted_iota(jnp.int32, (ny, rec), 0) + (slab * rows + i) * ny
        hit = jnp.where(line.astype(F32) == pack[STEPS + 1, 0:1, :], 1.0, 0.0).astype(BF16)
        hits = jnp.concatenate([hit, hit, hit], axis=1)

        def amount(q):
            return lax.dot_general(
                hits, targets[q], (((1,), (1,)), ((), ())), preferred_element_type=F32
            )

        def one(q, carry):
            sources[q, i] = amount(q)
            return carry

        lax.fori_loop(0, STEPS, one, 0)
        counts[i] = amount(STEPS)
        return carry

    lax.fori_loop(0, rows, spread, 0)
    spot[...] = jnp.where(
        (lax.broadcasted_iota(jnp.int32, (ny, nz), 0).astype(F32) == pack[STEPS + 1, 3:4, 0:nz])
        & (lax.broadcasted_iota(jnp.int32, (ny, nz), 1).astype(F32) == pack[STEPS + 1, 4:5, 0:nz]),
        1.0,
        0.0,
    )

    def face(buf, field, u, side):
        slot = lax.rem(u, 2)
        src = jnp.where(side == 0, 4, rows)
        dst = jnp.where(side == 0, rows + 4, 0)
        return pltpu.make_async_remote_copy(
            src_ref=buf.at[slot, pl.ds(src, 4), pl.ds(8, ny), :],
            dst_ref=buf.at[slot, pl.ds(dst, 4), pl.ds(8, ny), :],
            send_sem=halo_send.at[field, u, side],
            recv_sem=halo_recv.at[field, u, 1 - side],
            device_id=toward(side),
            device_id_type=MESH,
        )

    def arrival(buf, field, u, side):
        slot = lax.rem(u, 2)
        dst = jnp.where(side == 0, 0, rows + 4)
        block = buf.at[slot, pl.ds(dst, 4), pl.ds(8, ny), :]
        return pltpu.make_async_remote_copy(
            src_ref=block, dst_ref=block,
            send_sem=halo_send.at[field, u, side],
            recv_sem=halo_recv.at[field, u, side],
            device_id=toward(side),
            device_id_type=MESH,
        )

    def layer(buf, field, u, j):
        slot = lax.rem(u, 2)
        src = jnp.where(far_side == 0, 4 + j, rows + 3 - j)
        dst = jnp.where(far_side == 0, rows + 4 + j, 3 - j)
        return pltpu.make_async_remote_copy(
            src_ref=buf.at[slot, src, pl.ds(8, ny), :],
            dst_ref=buf.at[slot, dst, pl.ds(8, ny), :],
            send_sem=far_send.at[field, u, j],
            recv_sem=far_recv.at[field, u, j],
            device_id=toward(far_side),
            device_id_type=MESH,
        )

    def layer_arrival(buf, field, u, j):
        slot = lax.rem(u, 2)
        dst = jnp.where(far_side == 0, 3 - j, rows + 4 + j)
        place = buf.at[slot, dst, pl.ds(8, ny), :]
        return pltpu.make_async_remote_copy(
            src_ref=place, dst_ref=place,
            send_sem=far_send.at[field, u, j],
            recv_sem=far_recv.at[field, u, j],
            device_id=toward(far_side),
            device_id_type=MESH,
        )

    def send_near(buf, field, u):
        @pl.when(has(near_side))
        def _():
            face(buf, field, u, near_side).start()

    def send_all(buf, field):
        @pl.when(has(far_side))
        def _():
            for j in range(4):
                layer(buf, field, 0, j).start()

        send_near(buf, field, 0)

    def laplace(buf, slot, i, n):
        def at(x, y):
            return buf[slot, pl.ds(4 + i + x, n), 8 + y : 8 + y + ny, :]

        field = at(0, 0)
        high, middle, low = pieces(field.reshape(n * ny, nz))
        along = jnp.dot(
            jnp.concatenate([high, middle], axis=1), band[...], preferred_element_type=F32
        ) + jnp.dot(low, band[0:nz, :], preferred_element_type=F32)
        image = (3.0 * CENTRE) * field
        for index, weight in enumerate(COEFFS):
            k = index + 1
            image = image + weight * ((at(k, 0) + at(-k, 0)) + (at(0, k) + at(0, -k)))
        return field, image + along.reshape(n, ny, nz) * BAND_SCALE

    def advance(buf, field, u, plane):
        slot = lax.rem(u, 2)

        def run(first, count):
            def two(m, carry):
                plane(u, slot, first + 2 * m, 2)
                return carry

            lax.fori_loop(0, count // 2, two, 0)

        run(4, rows - 8)

        @pl.when(has(near_side))
        def _():
            arrival(buf, field, u, near_side).wait_recv()

            @pl.when(u > 0)
            def _():
                face(buf, field, u - 1, near_side).wait_send()

        run(jnp.where(near_side == 0, 0, rows - 4), 4)

        @pl.when(u < STEPS - 1)
        def _():
            send_near(buf, field, u + 1)

        even = lax.rem(u, 2) == 0

        def one(n, carry):
            j = jnp.where(even, 3 - n, n)

            @pl.when(has(far_side))
            def _():
                @pl.when(even)
                def _():
                    layer_arrival(buf, field, u, n).wait_recv()

                @pl.when(jnp.logical_and(jnp.logical_not(even), n == 0))
                def _():
                    for m in (3, 2, 1, 0):
                        layer_arrival(buf, field, u, m).wait_recv()

                @pl.when(u > 0)
                def _():
                    layer(buf, field, u - 1, j).wait_send()

            plane(u, slot, jnp.where(far_side == 0, j, rows - 1 - j), 1)

            @pl.when(jnp.logical_and(has(far_side), u < STEPS - 1))
            def _():
                layer(buf, field, u + 1, j).start()

            return carry

        lax.fori_loop(0, 4, one, 0)

    def settle(buf, field):
        @pl.when(has(near_side))
        def _():
            face(buf, field, STEPS - 1, near_side).wait_send()

        @pl.when(has(far_side))
        def _():
            for j in range(4):
                layer(buf, field, STEPS - 1, j).wait_send()

    def wave_plane(t, slot, i, n):
        now, image = laplace(wave, slot, i, n)
        here = pl.ds(i, n)
        inner = pl.ds(4 + i, n)
        position = (lax.broadcasted_iota(jnp.int32, (n, 1, nz), 0) + (slab * rows + i)).astype(F32)
        push = jnp.where(pack[STEPS + 1, 2:3, 0:nz] == position, pack[t, 1:2, 0:nz], 0.0)
        new = (
            2.0 * now - wave[1 - slot, inner, 8 : 8 + ny, :] + model[here] * image + push * spot[...]
        )
        source = counts[here] * new - sources[t, here]
        wave[1 - slot, inner, 8 : 8 + ny, :] = new
        images[t, here] = image
        sources[t, here] = source

    def adjoint_plane(u, slot, i, n):
        t = STEPS - 1 - u
        now, image = laplace(adj, slot, i, n)
        here = pl.ds(i, n)
        inner = pl.ds(4 + i, n)
        new = (
            2.0 * now - adj[1 - slot, inner, 8 : 8 + ny, :] + model[here] * image + sources[t, here]
        )
        gradient = grad[here] + new * images[t, here]
        adj[1 - slot, inner, 8 : 8 + ny, :] = new
        grad[here] = gradient

    fetched(1)
    send_all(wave, 0)
    fetched(3)

    def model_part(o, index, peer):
        return pltpu.make_async_remote_copy(
            src_ref=block(model, index), dst_ref=block(model, index),
            send_sem=model_send.at[o - 1], recv_sem=model_recv.at[o - 1],
            device_id={"shot": 2 * peer + core, "dom": dom}, device_id_type=MESH,
        )

    @pl.when(moves)
    def _():
        for o in range(1, groups):
            model_part(o, group, lax.rem(group + o, groups)).start()

    fetched(2)
    fetch(4, 5)

    @pl.when(moves)
    def _():
        for o in range(1, groups):
            origin = lax.rem(group + groups - o, groups)
            model_part(o, origin, origin).wait_recv()
            model_part(o, group, lax.rem(group + o, groups)).wait_send()

    def forward(t, carry):
        @pl.when(t == STEPS - 1)
        def _():
            fetched(4, 5)
            send_all(adj, 1)

        advance(wave, 0, t, wave_plane)
        return carry

    lax.fori_loop(0, STEPS, forward, 0)
    settle(wave, 0)

    def backward(u, carry):
        advance(adj, 1, u, adjoint_plane)
        return carry

    lax.fori_loop(0, STEPS, backward, 0)
    settle(adj, 1)

    def part(ref, index, n):
        return ref.at[pl.ds(index * chunk + n * depth, depth)]

    def to_across(q, n):
        return pltpu.make_async_remote_copy(
            src_ref=part(grad, q, n), dst_ref=part(other, q, n),
            send_sem=sum_send.at[q, n], recv_sem=sum_recv.at[q, n],
            device_id=across, device_id_type=MESH,
        )

    def to_group(o, n):
        peer = lax.rem(group + o, groups)
        return pltpu.make_async_remote_copy(
            src_ref=part(grad, peer, n), dst_ref=part(parts.at[o - 1], 0, n),
            send_sem=part_send.at[o - 1, n], recv_sem=part_recv.at[o - 1, n],
            device_id={"shot": 2 * peer + core, "dom": dom}, device_id_type=MESH,
        )

    def share(o, n, index, peer):
        return pltpu.make_async_remote_copy(
            src_ref=part(total, index, n), dst_ref=part(total, index, n),
            send_sem=all_send.at[o - 1, n], recv_sem=all_recv.at[o - 1, n],
            device_id={"shot": 2 * peer + core, "dom": dom}, device_id_type=MESH,
        )

    def to_core(o, n):
        index = lax.rem(group + groups - o, groups)
        return pltpu.make_async_remote_copy(
            src_ref=part(total, index, n), dst_ref=part(total, index, n),
            send_sem=core_send.at[o, n], recv_sem=core_recv.at[o, n],
            device_id=beside, device_id_type=MESH,
        )

    def top(n):
        return pltpu.make_async_remote_copy(
            src_ref=tops.at[dom], dst_ref=tops.at[dom],
            send_sem=top_send.at[n], recv_sem=top_recv.at[dom],
            device_id=member(n), device_id_type=MESH,
        )

    def top_arrival(d):
        return pltpu.make_async_remote_copy(
            src_ref=tops.at[d], dst_ref=tops.at[d],
            send_sem=top_send.at[0], recv_sem=top_recv.at[d],
            device_id=beside, device_id_type=MESH,
        )

    keep_model.wait()

    @pl.when(moves)
    def _():
        for n in range(pieces_of):
            for o in list(range(1, groups)) + [0]:
                to_across(lax.rem(group + o, groups), n).start()
        for n in range(pieces_of):
            to_core(0, n).wait_recv()
        for o in range(1, groups):
            for n in range(pieces_of):
                to_core(o, n).wait_recv()
        for n in range(pieces_of):
            for o in range(groups):
                to_across(o, n).wait_send()

    @pl.when(stays)
    def _():
        for n in range(pieces_of + 1):
            if n < pieces_of:
                for o in range(1, groups):
                    index = lax.rem(group + o, groups)
                    to_across(index, n).wait_recv()
                    for m in range(n * depth, n * depth + depth):
                        i = index * chunk + m
                        grad[i] = grad[i] + other[i]
                    to_group(o, n).start()
            if n > 0:
                last = n - 1
                to_across(group, last).wait_recv()
                for o in range(1, groups):
                    to_group(o, last).wait_recv()
                for m in range(last * depth, last * depth + depth):
                    i = group * chunk + m
                    value = grad[i] + other[i]
                    for o in range(1, groups):
                        value = value + parts[o - 1, m]
                    total[i] = value
                for o in range(1, groups):
                    share(o, last, group, lax.rem(group + o, groups)).start()
                to_core(0, last).start()
        for o in range(1, groups):
            origin = lax.rem(group + groups - o, groups)
            for n in range(pieces_of):
                share(o, n, origin, origin).wait_recv()
                to_core(o, n).start()

        def largest(i, best):
            return jnp.maximum(best, jnp.max(jnp.abs(total[i]).reshape(ny // 8, 8, nz), axis=0))

        tops[dom] = lax.fori_loop(0, rows, largest, jnp.zeros((8, nz), F32))

        def tell(n, carry):
            @pl.when(n != me)
            def _():
                top(n).start()

            return carry

        lax.fori_loop(0, 2 * doms, tell, 0)

    def hear(d, carry):
        @pl.when(jnp.logical_or(d != dom, moves))
        def _():
            top_arrival(d).wait_recv()

        return carry

    lax.fori_loop(0, doms, hear, 0)
    best = lax.fori_loop(0, doms, lambda d, b: jnp.maximum(b, tops[d]), jnp.zeros((8, nz), F32))
    divisor = jnp.max(best, keepdims=True) + EPSILON

    def finish(i, carry):
        direction = total[i] / divisor
        direction_ref[i] = direction
        new_model_ref[i] = own_model[i] * (1.0 - STEP_FRACTION * direction)
        return carry

    lax.fori_loop(0, rows, finish, 0)

    @pl.when(stays)
    def _():
        def told(n, carry):
            @pl.when(n != me)
            def _():
                top(n).wait_send()

            return carry

        lax.fori_loop(0, 2 * doms, told, 0)
        for n in range(pieces_of):
            for o in range(1, groups):
                to_group(o, n).wait_send()
                share(o, n, group, lax.rem(group + o, groups)).wait_send()
            for o in range(groups):
                to_core(o, n).wait_send()


def packed(rows, ny, nz, wavelet, source_cell, receiver_cells, observed):
    rec = receiver_cells.shape[1]
    zeros = jnp.zeros((STEPS, rec), F32)
    steps = jnp.stack(
        [observed[0], jnp.broadcast_to(wavelet[0][:, None], (STEPS, rec))] + [zeros] * 6, axis=1
    )
    cell = jnp.broadcast_to(source_cell[0], (rec,))
    receivers = receiver_cells[0]
    ones = jnp.stack([jnp.ones((rec,), F32)] + [zeros[0]] * 7)
    places = [receivers // nz, receivers % nz, cell // (ny * nz), cell // nz % ny, cell % nz]
    places = jnp.stack([p.astype(F32) for p in places] + [zeros[0]] * 3)
    return jnp.concatenate([steps, ones[None], places[None]], axis=0)


def on_device(
    shots, doms, model_slab, wave_prev, wave_now, adjoint_next, adjoint_now,
    wavelet, source_cell, receiver_cells, observed,
):
    rows, ny, nz = model_slab.shape
    rec = receiver_cells.shape[1]
    groups = shots // 2
    pack = packed(rows, ny, nz, wavelet, source_cell, receiver_cells, observed)
    dma = pltpu.SemaphoreType.DMA
    padded = (2, rows + 8, ny + 16, nz)
    slab = (rows, ny, nz)
    pieces_of = math.gcd(4, rows // groups)
    return pl.pallas_call(
        functools.partial(kernel, shots, doms),
        out_shape=(jax.ShapeDtypeStruct(slab, F32),) * 2,
        in_specs=[pl.BlockSpec(memory_space=pl.ANY)] * 6,
        out_specs=(pl.BlockSpec(memory_space=pltpu.VMEM),) * 2,
        scratch_shapes=[
            pltpu.VMEM(padded, F32),
            pltpu.VMEM(padded, F32),
            pltpu.VMEM((STEPS,) + slab, F32),
            pltpu.VMEM((STEPS,) + slab, F32),
            pltpu.VMEM(slab, F32),
            pltpu.VMEM(slab, F32),
            pltpu.VMEM(slab, F32),
            pltpu.VMEM(pack.shape, F32),
            pltpu.VMEM((STEPS + 1, nz, 3 * rec), BF16),
            pltpu.VMEM((2 * nz, nz), BF16),
            pltpu.VMEM((ny, nz), F32),
            pltpu.VMEM(slab, F32),
            pltpu.VMEM((groups - 1, rows // groups, ny, nz), F32),
            pltpu.VMEM(slab, F32),
            pltpu.VMEM(slab, F32),
            pltpu.VMEM((doms, 8, nz), F32),
            dma((6,)),
            dma((6,)),
            dma((2, STEPS, 2)),
            dma((2, STEPS, 2)),
            dma((2, STEPS, 4)),
            dma((2, STEPS, 4)),
            dma((groups - 1,)),
            dma((groups - 1,)),
            dma((groups, pieces_of)),
            dma((groups, pieces_of)),
            dma((groups - 1, pieces_of)),
            dma((groups - 1, pieces_of)),
            dma((groups - 1, pieces_of)),
            dma((groups - 1, pieces_of)),
            dma((groups, pieces_of)),
            dma((groups, pieces_of)),
            dma((2 * doms,)),
            dma((doms,)),
            dma((1,)),
        ],
        compiler_params=pltpu.CompilerParams(
            collective_id=0, has_side_effects=True, vmem_limit_bytes=60 * 1024 * 1024
        ),
    )(pack, model_slab, wave_prev[0], wave_now[0], adjoint_next[0], adjoint_now[0])


def solution(mesh):
    placed = (
        P("dom", None, None),
        P("shot", "dom", None, None),
        P("shot", "dom", None, None),
        P("shot", "dom", None, None),
        P("shot", "dom", None, None),
        P("shot", None),
        P("shot"),
        P("shot", None),
        P("shot", None, None),
    )
    return jax.shard_map(
        functools.partial(on_device, mesh.shape["shot"], mesh.shape["dom"]),
        mesh=mesh,
        in_specs=placed,
        out_specs=(P("dom", None, None), P("dom", None, None)),
        check_vma=False,
    )
```
